512 devices in a mesh: tile: 32 (over x, z_hi, y), tag: 16 (over z_lo, core).
Axes of the slice: x: 4, y: 4, z: 16 (z_hi: 2, z_lo: 8; z = z_hi * 8 + z_lo), core: 2. Of those that a mesh axis runs over, the one named last changes fastest.
Arguments:
- tracers: float32 [96, 8, 8, 6144], P('tile', None, None, 'tag'), may hold values from 0.05 to 5
- eastward_mass: float32 [96, 8, 9, 64], P('tile', None, None, 'tag'), may hold values from -0.15 to 0.15
- eastward_courant: float32 [96, 8, 9, 64], P('tile', None, None, 'tag'), may hold values from -0.9 to 0.9
- northward_mass: float32 [96, 9, 8, 64], P('tile', None, None, 'tag'), may hold values from -0.15 to 0.15
- northward_courant: float32 [96, 9, 8, 64], P('tile', None, None, 'tag'), may hold values from -0.9 to 0.9
- thickness: float32 [96, 8, 8, 64], P('tile', None, None, 'tag'), may hold values from 1 to 2
- neighbor: int32 [96, 4], replicated, may hold values from 0 to 95, as said below
- orientation: int32 [96, 4], replicated, may hold values from 0 to 7, as said below
Outputs:
- tracers_next: float32 [96, 8, 8, 6144], P('tile', None, None, 'tag')
The draws below stay inside these ranges and needn't reach their ends.
Inputs may be any that keep to these rules, and one draw needn't show every extreme that they name: The tiles are those of a cube surface of 6 faces of 4 x 4 tiles, numbered in an arbitrary order, each with its own right-handed cell frame in one of four quarter-turn orientations; neighbor and orientation describe which side of which tile meets each side, and the matching is symmetric. orientation[t, s] = 2 s' + f, with s' the side of tile neighbor[t, s] that meets side s of t, and f = 1 where the two tiles number the cells along that edge in opposite directions.
All inputs are finite; a program needn't handle non-finite values.
Results may differ from the reference program's by a relative error of at most 0.0003.
Values sent between devices are 32-bit elements; how exact they have to be, the bound alone decides.
A program may use at most 128 MiB of HBM per device.

```python
import math
import jax
import jax.numpy as jnp
import numpy as np
from jax import lax

SUB = 4
C = 8
TAGS = 96
LEV = 64
NTILES = 96


def cube_tables():
    frames = [((1, 0, 0), (0, 1, 0), (0, 0, 1)), ((-1, 0, 0), (0, 0, 1), (0, 1, 0)), ((0, 1, 0), (0, 0, 1), (1, 0, 0)), ((0, -1, 0), (1, 0, 0), (0, 0, 1)), ((0, 0, 1), (1, 0, 0), (0, 1, 0)), ((0, 0, -1), (0, 1, 0), (1, 0, 0))]
    count_tiles = 6 * SUB * SUB
    found = {}
    for face_number in range(6):
        normal_vec = np.array(frames[face_number][0], dtype=np.int32)
        axis_first = np.array(frames[face_number][1], dtype=np.int32)
        axis_second = np.array(frames[face_number][2], dtype=np.int32)
        for tile_row in range(SUB):
            for tile_col in range(SUB):
                canon = face_number * SUB * SUB + tile_row * SUB + tile_col
                col_low = -2 * SUB + 4 * tile_col
                row_low = -2 * SUB + 4 * tile_row
                spots = [(col_low, row_low + 2), (col_low + 4, row_low + 2), (col_low + 2, row_low), (col_low + 2, row_low + 4)]
                for side_number in range(4):
                    coord_first = spots[side_number][0]
                    coord_second = spots[side_number][1]
                    point = 2 * SUB * normal_vec + coord_first * axis_first + coord_second * axis_second
                    label = (int(point[0]), int(point[1]), int(point[2]))
                    if label in found:
                        found[label] = found[label] + [(canon, side_number)]
                    else:
                        found[label] = [(canon, side_number)]
    partner_tile = np.zeros((count_tiles, 4), dtype=np.int32)
    partner_side = np.zeros((count_tiles, 4), dtype=np.int32)
    for label in found:
        pairs = found[label]
        tile_one, side_one = pairs[0]
        tile_two, side_two = pairs[1]
        partner_tile[tile_one, side_one] = tile_two
        partner_side[tile_one, side_one] = side_two
        partner_tile[tile_two, side_two] = tile_one
        partner_side[tile_two, side_two] = side_one
    return (partner_tile, partner_side)


def draw_matching(key):
    count_tiles = 6 * SUB * SUB
    partner_tile, partner_side = cube_tables()
    cyclic = jnp.array([2, 0, 3, 1], dtype=jnp.int32)
    uncyclic = jnp.array([1, 3, 0, 2], dtype=jnp.int32)
    direction = jnp.array([1, -1, -1, 1], dtype=jnp.int32)
    key_perm, key_turn = jax.random.split(key)
    labels = jax.random.permutation(key_perm, count_tiles).astype(jnp.int32)
    turns = jax.random.randint(key_turn, (count_tiles,), 0, 4).astype(jnp.int32)
    local_sides = jnp.arange(4, dtype=jnp.int32)[None, :]
    canon_side = uncyclic[(cyclic[local_sides] + turns[:, None]) % 4]
    canon_rows = jnp.arange(count_tiles, dtype=jnp.int32)[:, None]
    other_tile = jnp.asarray(partner_tile)[canon_rows, canon_side]
    other_canon_side = jnp.asarray(partner_side)[canon_rows, canon_side]
    other_side = uncyclic[(cyclic[other_canon_side] - turns[other_tile]) % 4]
    flipped = (direction[cyclic[local_sides]] == direction[cyclic[other_side]]).astype(jnp.int32)
    neighbor_canon = labels[other_tile]
    orient_canon = 2 * other_side + flipped
    neighbor = jnp.zeros((count_tiles, 4), jnp.int32).at[labels].set(neighbor_canon)
    orientation = jnp.zeros((count_tiles, 4), jnp.int32).at[labels].set(orient_canon)
    return (neighbor, orientation)


def draw_neighbor(key, part):
    tables = draw_matching(key)
    return tables[0]


def draw_orientation(key, part):
    tables = draw_matching(key)
    return tables[1]


def shard_levels(rng, extent, cuts, least, high):
    level, own = 1.0, jax.random.fold_in(rng, 6)
    for position, shards_of in cuts:
        draws = jnp.exp(jax.random.uniform(jax.random.fold_in(own, position), (shards_of,), jnp.float32, least / len(cuts), high / len(cuts)))
        level = level * jnp.repeat(draws, extent[position] // shards_of).reshape([-1 if axis == position else 1 for axis in range(len(extent))])
    return level


def setup_inputs(seed: int = 0) -> dict:
    key_list = jax.random.split(jax.random.key(seed), 9)
    return {
        "tracers": jnp.clip(jnp.exp(math.log(5.0) - 4.6051702 * jax.random.uniform(key_list[0], (NTILES, C, C, TAGS * LEV), jnp.float32) ** shard_levels(key_list[0], (NTILES, C, C, TAGS * LEV), ((0, 32), (3, 16)), -0.2, 0.2)), 0.05, 5.0),
        "eastward_mass": jnp.clip(jax.random.uniform(key_list[1], (NTILES, C, C + 1, LEV), jnp.float32, -0.15, 0.15) * shard_levels(key_list[1], (NTILES, C, C + 1, LEV), ((0, 32), (3, 16)), -0.4, 0.0), -0.15, 0.15),
        "eastward_courant": jnp.clip(jax.random.uniform(key_list[2], (NTILES, C, C + 1, LEV), jnp.float32, -0.9, 0.9) * shard_levels(key_list[2], (NTILES, C, C + 1, LEV), ((0, 32), (3, 16)), -0.4, 0.0), -0.9, 0.9),
        "northward_mass": jnp.clip(jax.random.uniform(key_list[3], (NTILES, C + 1, C, LEV), jnp.float32, -0.15, 0.15) * shard_levels(key_list[3], (NTILES, C + 1, C, LEV), ((0, 32), (3, 16)), -0.4, 0.0), -0.15, 0.15),
        "northward_courant": jnp.clip(jax.random.uniform(key_list[4], (NTILES, C + 1, C, LEV), jnp.float32, -0.9, 0.9) * shard_levels(key_list[4], (NTILES, C + 1, C, LEV), ((0, 32), (3, 16)), -0.4, 0.0), -0.9, 0.9),
        "thickness": jnp.clip(1.0 + 1.0 * jax.random.uniform(key_list[5], (NTILES, C, C, LEV), jnp.float32) ** shard_levels(key_list[5], (NTILES, C, C, LEV), ((0, 32), (3, 16)), -0.2, 0.2), 1.0, 2.0),
        "neighbor": draw_neighbor(jax.random.fold_in(key_list[8], 71), 0),
        "orientation": draw_orientation(jax.random.fold_in(key_list[8], 71), 0),
    }


seven_twelfths = 7.0 / 12.0
one_twelfth = 1.0 / 12.0


def edge_strips(tile_cells):
    west_side = jnp.stack([tile_cells[:, :, 0], tile_cells[:, :, 1]], 1)
    east_side = jnp.stack([tile_cells[:, :, -1], tile_cells[:, :, -2]], 1)
    south_side = jnp.stack([tile_cells[:, 0], tile_cells[:, 1]], 1)
    north_side = jnp.stack([tile_cells[:, -1], tile_cells[:, -2]], 1)
    return jnp.stack([west_side, east_side, south_side, north_side], 1)


def face_flux(wide_cells, mass_face, courant_face, along_axis, edge_cells):
    outer_low = lax.slice_in_dim(wide_cells, 0, edge_cells + 1, axis=along_axis)
    inner_low = lax.slice_in_dim(wide_cells, 1, edge_cells + 2, axis=along_axis)
    inner_high = lax.slice_in_dim(wide_cells, 2, edge_cells + 3, axis=along_axis)
    outer_high = lax.slice_in_dim(wide_cells, 3, edge_cells + 4, axis=along_axis)
    mass_wide = mass_face[:, :, :, None, :]
    courant_wide = courant_face[:, :, :, None, :]
    face_value = seven_twelfths * (inner_low + inner_high) - one_twelfth * (outer_low + outer_high)
    return mass_wide * (face_value - 0.5 * courant_wide * (inner_high - inner_low))


def advance_tiles(tile_cells, halo_cells, eastward_mass, eastward_courant, northward_mass, northward_courant, thickness):
    edge_cells = tile_cells.shape[1]
    west_cols = jnp.stack([halo_cells[:, 0, 1], halo_cells[:, 0, 0]], 2)
    east_cols = jnp.stack([halo_cells[:, 1, 0], halo_cells[:, 1, 1]], 2)
    south_rows = jnp.stack([halo_cells[:, 2, 1], halo_cells[:, 2, 0]], 1)
    north_rows = jnp.stack([halo_cells[:, 3, 0], halo_cells[:, 3, 1]], 1)
    wide_along = jnp.concatenate([west_cols, tile_cells, east_cols], 2)
    wide_across = jnp.concatenate([south_rows, tile_cells, north_rows], 1)
    flux_along = face_flux(wide_along, eastward_mass, eastward_courant, 2, edge_cells)
    flux_across = face_flux(wide_across, northward_mass, northward_courant, 1, edge_cells)
    divergence = flux_along[:, :, 1:] - flux_along[:, :, :-1] + flux_across[:, 1:] - flux_across[:, :-1]
    mass_change = eastward_mass[:, :, 1:] - eastward_mass[:, :, :-1] + northward_mass[:, 1:] - northward_mass[:, :-1]
    new_thickness = thickness - mass_change
    return (tile_cells * thickness[:, :, :, None, :] - divergence) / new_thickness[:, :, :, None, :]


def reference(tracers, eastward_mass, eastward_courant, northward_mass, northward_courant, thickness, neighbor, orientation):
    tile_cells = tracers.reshape(NTILES, C, C, TAGS, LEV)
    strips = edge_strips(tile_cells)

    def one_tile(tile_index):
        partner = neighbor[tile_index].astype(jnp.int32)
        code = orientation[tile_index].astype(jnp.int32)
        picked = strips[partner, code // 2]
        turned = jnp.flip(picked, 2)
        halo_cells = jnp.where((code % 2 == 1)[:, None, None, None, None], turned, picked)
        stepped = advance_tiles(tile_cells[tile_index][None], halo_cells[None], eastward_mass[tile_index][None], eastward_courant[tile_index][None], northward_mass[tile_index][None], northward_courant[tile_index][None], thickness[tile_index][None])
        return stepped[0]

    stepped_all = lax.map(one_tile, jnp.arange(NTILES).astype(jnp.int32))
    return stepped_all.reshape(NTILES, C, C, TAGS * LEV)
```

```python
import jax
import jax.numpy as jnp
from jax import lax
from jax.experimental import pallas as pl
from jax.experimental.pallas import tpu as pltpu
from jax.sharding import PartitionSpec as P

MESH = pl.DeviceIdType.MESH
T = 3
C = 8
K = 16
Z = 8
CH = 3
ROWS = 9
SIDES = 12
FW = 384


def collector_cells(k):
    cy, cx, dy, dx = k // 8, k // 4 % 2, k // 2 % 2, k % 2
    far = lambda flag, d: 7 - d if flag else d
    corner = (far(cy, dy), far(cx, dx))
    across_x = (5 - dy if cy else 2 + dy, far(1 - cx, dx))
    across_y = (far(1 - cy, dy), 5 - dx if cx else 2 + dx)
    return corner, across_x, across_y


def kernel(q, mx, cx_ref, my, cy_ref, th, nbr, ori, out, s1, r1a, r1b, r1c, s2, r2a, r2b, r2c, halo, flow, wide, grid,
           acc, kx, ky, pick, place, ready, ssem1, rsem1, ssem2, rsem2, fright, fleft, fsend, fcore, fcsend):
    r1, r2 = (r1a, r1b, r1c), (r2a, r2b, r2c)
    tile, tag = lax.axis_index("tile"), lax.axis_index("tag")
    x, half, y = tile // 8, lax.rem(tile // 4, 2), lax.rem(tile, 4)
    me = x * 4 + y
    z, core = tag // 2, lax.rem(tag, 2)
    cy, cx = me // 8, lax.rem(me // 4, 2)

    def member(k, h):
        return ((k // 4) * 8 + h * 4 + lax.rem(k, 4), tag)

    def line(zz):
        return (tile, zz * 2 + core)

    twin = (tile, z * 2 + 1 - core)
    barrier = pltpu.get_barrier_semaphore()

    def greet(dev):
        pl.semaphore_signal(barrier, inc=1, device_id=dev, device_id_type=MESH)

    def greet_plane(i, carry):
        greet(member(lax.rem(me + i, K), half))
        return carry

    lax.fori_loop(1, K, greet_plane, 0)
    greet(twin)

    @pl.when(z > 0)
    def _():
        greet(line(z - 1))

    @pl.when(z < Z - 1)
    def _():
        greet(line(z + 1))

    def all_rows(ref, sem, rows):
        pltpu.make_async_copy(ref.at[pl.ds(0, rows)], ref.at[pl.ds(0, rows)], sem).wait()

    def stage(t, carry):
        for k in range(K):
            for slot, (j, i) in enumerate(collector_cells(k)):
                for c in range(CH):
                    s1[c, k, t * 3 + slot] = q[t, j, i:i + 1, c * 128:(c + 1) * 128]
        return carry

    lax.fori_loop(0, T, stage, 0)

    near = K + jnp.where(z > 0, 1, 0) + jnp.where(z < Z - 1, 1, 0)

    @pl.when(half == 0)
    def _():
        pl.semaphore_wait(barrier, near)

        def greet_far(i, carry):
            greet(member(lax.rem(me + i, K), 1))
            return carry

        lax.fori_loop(0, K, greet_far, 0)

    def first_copy(c, k, h):
        return pltpu.make_async_remote_copy(
            src_ref=s1.at[c, k], dst_ref=r1[c].at[pl.ds(tile * ROWS, ROWS)], send_sem=ssem1.at[c],
            recv_sem=rsem1.at[c], device_id=member(k, h), device_id_type=MESH)

    def send_far():
        for c in range(CH):
            def go(i, carry, c=c):
                first_copy(c, lax.rem(me + i, K), 1 - half).start()
                return carry

            lax.fori_loop(0, K, go, 0)

    @pl.when(half == 1)
    def _():
        pl.semaphore_wait(barrier, near + K)

        def answer(i, carry):
            pl.semaphore_signal(ready, inc=1, device_id=member(lax.rem(me + i, K), 0), device_id_type=MESH)
            return carry

        lax.fori_loop(0, K, answer, 0)
        send_far()

    for c in range(CH):
        def go(i, carry, c=c):
            first_copy(c, lax.rem(me + i, K), half).start()
            return carry

        lax.fori_loop(1, K, go, 0)
        r1[c][pl.ds(tile * ROWS, ROWS)] = s1[c, me]

    def pack(t, carry):
        flow[tag, t] = jnp.zeros((4, FW), jnp.float32)
        for j in range(C):
            for n, ref in enumerate((mx, cx_ref, my, cy_ref)):
                at = n * 72 + j * 9
                flow[tag, t, :, at:at + 9] = ref[t, j]
            at = 288 + j * 8
            flow[tag, t, :, at:at + 8] = th[t, j]
        return carry

    lax.fori_loop(0, T, pack, 0)

    def block(zz):
        return flow.at[zz * 2 + core]

    def pass_on(zz, dev, sem, done):
        return pltpu.make_async_remote_copy(src_ref=block(zz), dst_ref=block(zz), send_sem=done, recv_sem=sem,
                                            device_id=dev, device_id_type=MESH)

    for s in range(Z):
        for way, step, sems, here, inner in ((0, -1, fright, z >= s, z < Z - 1), (1, 1, fleft, z + s < Z, z > 0)):
            zz = z + step * s
            if s == 0 and step == -1:
                pass_on(z, twin, fcore, fcsend).start()
            if s:
                @pl.when(here)
                def _():
                    pass_on(zz, twin, sems.at[s - 1], fcsend).wait_recv()
                    pass_on(zz, twin, fcore, fcsend).start()

            if s < Z - 1:
                @pl.when(here & inner)
                def _():
                    pass_on(zz, line(z - step), sems.at[s], fsend.at[way, s]).start()

    @pl.when(half == 0)
    def _():
        pl.semaphore_wait(ready, K)
        send_far()

    def find(n, carry):
        k, r = n // SIDES, lax.rem(n, SIDES)
        t, s = r // 4, lax.rem(r, 4)
        home = ((k // 4) * 8 + half * 4 + lax.rem(k, 4)) * T + t
        side = ori[s, home] // 2
        b = lax.rem(side, 2)
        slot = jnp.where(side // 2 == 1, jnp.where(b == cy, 0, 2), jnp.where(b == cx, 0, 1))
        pick[n] = nbr[s, home] * 3 + slot
        return carry

    lax.fori_loop(0, K * SIDES, find, 0)

    def locate(r, carry):
        t, s = r // 4, lax.rem(r, 4)
        code = ori[s, tile * T + t]
        flip, b, is_y = lax.rem(code, 2), lax.rem(code // 2, 2), code // 4
        for d in range(2):
            for a in range(C):
                a2, a1, a0 = a // 4, a // 2 % 2, a % 2
                end = 1 - flip if a2 else flip
                cross = 1 - b if a1 != a2 else b
                deep = a0 ^ a2
                kx_at = end * 8 + cross * 4 + deep * 2 + d
                ky_at = cross * 8 + end * 4 + d * 2 + deep
                place[r * 16 + d * 8 + a] = jnp.where(is_y == 1, ky_at, kx_at) * SIDES + r
        return carry

    lax.fori_loop(0, SIDES, locate, 0)

    all_rows(flow, fcore, Z)

    def turn(t, carry):
        for g in range(2 * Z):
            wide[4 * g:4 * g + 4, :] = flow[g, t]
            wide[64 + 4 * g:68 + 4 * g, :] = flow[g, t]
        for p in range(FW // 128):
            grid[t, p * 128:(p + 1) * 128, :] = wide[:, p * 128:(p + 1) * 128].T
        return carry

    lax.fori_loop(0, T, turn, 0)

    row = lax.broadcasted_iota(jnp.int32, (C, 128), 0)

    def stencil(m_low, c_low, m_high, c_high, scale):
        m_low, m_high = m_low * scale, m_high * scale
        low, high = m_low * (1.0 / 12.0), m_high * (1.0 / 12.0)
        return (
            -low,
            m_low * (7.0 / 12.0 + 0.5 * c_low) + high,
            m_low * (7.0 / 12.0 - 0.5 * c_low) - m_high * (7.0 / 12.0 + 0.5 * c_high),
            -m_high * (7.0 / 12.0 - 0.5 * c_high) - low,
            high,
        )

    def inner_step(t, carry):
        for j in range(C):
            x_low, x_high = grid[t, 9 * j:9 * j + 8, :], grid[t, 9 * j + 1:9 * j + 9, :]
            xc_low, xc_high = grid[t, 72 + 9 * j:80 + 9 * j, :], grid[t, 73 + 9 * j:81 + 9 * j, :]
            y_low, y_high = grid[t, pl.ds(144 + j, 8, stride=9), :], grid[t, pl.ds(145 + j, 8, stride=9), :]
            yc_low, yc_high = grid[t, pl.ds(216 + j, 8, stride=9), :], grid[t, pl.ds(217 + j, 8, stride=9), :]
            thick = grid[t, 288 + 8 * j:296 + 8 * j, :]
            scale = 1.0 / (thick - (x_high - x_low + y_high - y_low))
            xs = stencil(x_low, xc_low, x_high, xc_high, scale)
            ys = stencil(y_low, yc_low, y_high, yc_high, scale)
            centre = thick * scale + xs[2] + ys[2]
            for n, (v, i) in enumerate(((xs[1], 0), (xs[0], 0), (xs[0], 1), (xs[3], 7), (xs[4], 7), (xs[4], 6))):
                kx[t, n, j:j + 1, :] = v[i:i + 1, :]
            for n, (v, at) in enumerate(((ys[1], 0), (ys[0], 0), (ys[0], 1), (ys[3], 7), (ys[4], 7), (ys[4], 6))):
                if at == j:
                    ky[t, n] = v
            xm2 = jnp.where(row >= 2, xs[0], 0.0)
            xm1 = jnp.where(row >= 1, xs[1], 0.0)
            xp1 = jnp.where(row <= 6, xs[3], 0.0)
            xp2 = jnp.where(row <= 5, xs[4], 0.0)
            for c in range(CH):
                lanes = slice(c * 128, (c + 1) * 128)
                v = q[t, j, :, lanes]
                total = centre * v
                total += xm2 * pltpu.roll(v, 2, 0) + xm1 * pltpu.roll(v, 1, 0)
                total += xp1 * pltpu.roll(v, 7, 0) + xp2 * pltpu.roll(v, 6, 0)
                for step, w in ((-2, ys[0]), (-1, ys[1]), (1, ys[3]), (2, ys[4])):
                    if 0 <= j + step < C:
                        total += w * q[t, j + step, :, lanes]
                acc[c, t, 8 * j:8 * j + 8, :] = total
        return carry

    lax.fori_loop(0, T, inner_step, 0)

    def second_copy(c, k):
        return pltpu.make_async_remote_copy(
            src_ref=s2.at[c, k], dst_ref=r2[c].at[pl.ds(me * SIDES, SIDES)], send_sem=ssem2.at[c],
            recv_sem=rsem2.at[c], device_id=member(k, half), device_id_type=MESH)

    def collect(c):
        all_rows(r1[c], rsem1.at[c], (2 * K - 1) * ROWS)

        def choose(k, carry):
            for r in range(SIDES):
                s2[c, k, r] = r1[c][pick[k * SIDES + r]]
            return carry

        lax.fori_loop(0, K, choose, 0)

        def go(i, carry):
            second_copy(c, lax.rem(me + i, K)).start()
            return carry

        lax.fori_loop(1, K, go, 0)
        r2[c][pl.ds(me * SIDES, SIDES)] = s2[c, me]

    def finish(c):
        all_rows(r2[c], rsem2.at[c], (K - 1) * SIDES)

        def lay(r, carry):
            for d in range(2):
                for a in range(C):
                    halo[r, d, a:a + 1, :] = r2[c][place[r * 16 + d * 8 + a]]
            return carry

        lax.fori_loop(0, SIDES, lay, 0)

        def add(t, carry):
            west, east, south, north = ((halo[t * 4 + s, 0], halo[t * 4 + s, 1]) for s in range(4))
            for (one, two), n, edge, inside in ((west, 0, 0, 1), (east, 3, 7, 6)):
                acc[c, t, pl.ds(edge, 8, stride=8), :] += kx[t, n] * one + kx[t, n + 1] * two
                acc[c, t, pl.ds(inside, 8, stride=8), :] += kx[t, n + 2] * one
            for (one, two), n, edge, inside in ((south, 0, 0, 1), (north, 3, 7, 6)):
                acc[c, t, 8 * edge:8 * edge + 8, :] += ky[t, n] * one + ky[t, n + 1] * two
                acc[c, t, 8 * inside:8 * inside + 8, :] += ky[t, n + 2] * one
            for j in range(C):
                out[t, j, :, c * 128:(c + 1) * 128] = acc[c, t, 8 * j:8 * j + 8, :]
            return carry

        lax.fori_loop(0, T, add, 0)

    for c in range(CH):
        collect(c)
        if c:
            finish(c - 1)
    finish(CH - 1)

    for c in range(CH):
        all_rows(r1[c], ssem1.at[c], (2 * K - 1) * ROWS)
        all_rows(r2[c], ssem2.at[c], (K - 1) * SIDES)
    all_rows(flow, fcsend, Z)
    for s in range(Z - 1):
        for way, here in ((0, (z >= s) & (z < Z - 1)), (1, (z + s < Z) & (z > 0))):
            @pl.when(here)
            def _():
                pass_on(z, twin, fcore, fsend.at[way, s]).wait_send()


def shards(tracers, eastward_mass, eastward_courant, northward_mass, northward_courant, thickness, neighbor, orientation):
    f32 = jnp.float32
    vmem, smem = pl.BlockSpec(memory_space=pltpu.VMEM), pl.BlockSpec(memory_space=pltpu.SMEM)
    dma = pltpu.SemaphoreType.DMA
    return pl.pallas_call(
        kernel,
        out_shape=jax.ShapeDtypeStruct(tracers.shape, f32),
        in_specs=[vmem] * 6 + [smem] * 2,
        out_specs=vmem,
        scratch_shapes=[
            pltpu.VMEM((CH, K, ROWS, 1, 128), f32),
            *[pltpu.VMEM((2 * K * ROWS, 1, 128), f32)] * CH,
            pltpu.VMEM((CH, K, SIDES, 1, 128), f32),
            *[pltpu.VMEM((K * SIDES, 1, 128), f32)] * CH,
            pltpu.VMEM((SIDES, 2, C, 128), f32),
            pltpu.VMEM((2 * Z, T, 4, FW), f32),
            pltpu.VMEM((128, FW), f32),
            pltpu.VMEM((T, FW, 128), f32),
            pltpu.VMEM((CH, T, C * C, 128), f32),
            pltpu.VMEM((T, 6, C, 128), f32),
            pltpu.VMEM((T, 6, C, 128), f32),
            pltpu.SMEM((K * SIDES,), jnp.int32),
            pltpu.SMEM((SIDES * 16,), jnp.int32),
            pltpu.SemaphoreType.REGULAR,
            dma((CH,)), dma((CH,)), dma((CH,)), dma((CH,)),
            dma((Z,)), dma((Z,)), dma((2, Z)), dma, dma,
        ],
        compiler_params=pltpu.CompilerParams(collective_id=0, has_side_effects=True, vmem_limit_bytes=32 * 2**20),
    )(
        tracers,
        eastward_mass.transpose(0, 1, 3, 2),
        eastward_courant.transpose(0, 1, 3, 2),
        northward_mass.transpose(0, 2, 3, 1),
        northward_courant.transpose(0, 2, 3, 1),
        thickness.transpose(0, 1, 3, 2),
        neighbor.T,
        orientation.T,
    )


def solution(mesh):
    split = P("tile", None, None, "tag")
    return jax.shard_map(
        shards,
        mesh=mesh,
        in_specs=(split,) * 6 + (P(), P()),
        out_specs=split,
        check_vma=False,
    )
```

```python
import jax
import jax.numpy as jnp
from jax import lax
from jax.experimental import pallas as pl
from jax.experimental.pallas import tpu as pltpu
from jax.sharding import PartitionSpec as P

MESH = pl.DeviceIdType.MESH
T = 3
C = 8
REACH = 4
K = 16
Z = 8
CH = 3
ROWS = 9
SIDES = 12
FW = 384


def collector_cells(k):
    cy, cx, dy, dx = k // 8, k // 4 % 2, k // 2 % 2, k % 2
    far = lambda flag, d: 7 - d if flag else d
    corner = (far(cy, dy), far(cx, dx))
    across_x = (5 - dy if cy else 2 + dy, far(1 - cx, dx))
    across_y = (far(1 - cy, dy), 5 - dx if cx else 2 + dx)
    return corner, across_x, across_y


def kernel(q_in, mx_in, cx_in, my_in, cy_in, th_in, nbr_in, ori_in, out, q, mx, cx_ref, my, cy_ref, th, nbr, ori, load, s1, r1a, r1b, r1c, s2, r2a, r2b, r2c, halo, flow, wide, grid,
           acc, kx, ky, pick_v, place_v, pick, place, ready, ssem1, rsem1, ssem2, rsem2, fnear, fsend, fcore, fcsend):
    r1, r2 = (r1a, r1b, r1c), (r2a, r2b, r2c)
    tile, tag = lax.axis_index("tile"), lax.axis_index("tag")
    x, half, y = tile // 8, lax.rem(tile // 4, 2), lax.rem(tile, 4)
    me = x * 4 + y
    z, core = tag // 2, lax.rem(tag, 2)
    cy, cx = me // 8, lax.rem(me // 4, 2)

    def line(zz):
        return (tile, zz * 2 + core)

    inputs = [
        pltpu.make_async_copy(src, dst, load.at[n]) for n, (src, dst) in enumerate((
            (q_in, q), (mx_in, mx), (cx_in, cx_ref), (my_in, my), (cy_in, cy_ref), (th_in, th), (nbr_in, nbr), (ori_in, ori)))]
    for copy in inputs:
        copy.start()

    twin = (tile, z * 2 + 1 - core)
    barrier = pltpu.get_barrier_semaphore()

    def greet(dev):
        pl.semaphore_signal(barrier, inc=1, device_id=dev, device_id_type=MESH)

    xs = [jnp.where(x + i < 4, x + i, x + i - 4) for i in range(4)]
    ys = [jnp.where(y + i < 4, y + i, y + i - 4) for i in range(4)]
    ring = [(xs[i // 4] * 4 + ys[i % 4], xs[i // 4] * 8 + ys[i % 4]) for i in range(K)]

    def device(i, h):
        return (ring[i][1] + h * 4, tag)

    for i in range(1, K):
        greet(device(i, half))
    greet(twin)

    @pl.when(half == 0)
    def _():
        for i in range(K):
            greet(device(i, 1))

    def on_line(zz):
        return (zz >= 0) & (zz < Z)

    for d in range(1, REACH + 1):
        for way in (-1, 1):
            @pl.when(on_line(z + way * d))
            def _():
                greet(line(z + way * d))

    near = K + jnp.minimum(z, REACH) + jnp.minimum(Z - 1 - z, REACH)

    def all_rows(ref, sem, rows):
        pltpu.make_async_copy(ref.at[pl.ds(0, rows)], ref.at[pl.ds(0, rows)], sem).wait()

    inputs[6].wait()
    inputs[7].wait()
    code = ori[...]
    flip, b, is_y = code & 1, (code >> 1) & 1, code >> 2 == 1
    slot = jnp.where(is_y, jnp.where(b == cy, 0, 2), jnp.where(b == cx, 0, 1))
    pick_v[...] = nbr[...] * 3 + slot
    side_row = lax.broadcasted_iota(jnp.int32, (4, 32 * T), 0)
    for d in range(2):
        for a in range(C):
            a2, a1, a0 = a // 4, a // 2 % 2, a % 2
            end = 1 - flip if a2 else flip
            cross = 1 - b if a1 != a2 else b
            deep = a0 ^ a2
            kx_at = end * 8 + cross * 4 + deep * 2 + d
            ky_at = cross * 8 + end * 4 + d * 2 + deep
            place_v[d * 8 + a] = jnp.where(is_y, ky_at, kx_at) * SIDES + side_row
    tables = [pltpu.make_async_copy(pick_v, pick, load.at[8]), pltpu.make_async_copy(place_v, place, load.at[9])]
    for copy in tables:
        copy.start()

    def stage(t, carry):
        for k in range(K):
            for slot, (j, i) in enumerate(collector_cells(k)):
                for c in range(CH):
                    s1[c, k, t * 3 + slot] = q[t, j, i:i + 1, c * 128:(c + 1) * 128]
        return carry

    inputs[0].wait()
    lax.fori_loop(0, T, stage, 0)

    def first_copy(c, i, h):
        return pltpu.make_async_remote_copy(
            src_ref=s1.at[c, ring[i][0]], dst_ref=r1[c].at[pl.ds(tile * ROWS, ROWS)], send_sem=ssem1.at[c],
            recv_sem=rsem1.at[c], device_id=device(i, h), device_id_type=MESH)

    def send_far():
        for c in range(CH):
            for i in range(K):
                first_copy(c, i, 1 - half).start()

    def pack(t, carry):
        flow[tag, t] = jnp.zeros((4, FW), jnp.float32)
        for j in range(C):
            for n, ref in enumerate((mx, cx_ref, my, cy_ref)):
                at = n * 72 + j * 9
                flow[tag, t, :, at:at + 9] = ref[t, j]
            at = 288 + j * 8
            flow[tag, t, :, at:at + 8] = th[t, j]
        return carry

    for copy in inputs[1:6]:
        copy.wait()
    lax.fori_loop(0, T, pack, 0)

    def block(zz):
        return flow.at[zz * 2 + core]

    def pass_on(zz, dev, sem, done):
        return pltpu.make_async_remote_copy(src_ref=block(zz), dst_ref=block(zz), send_sem=done, recv_sem=sem,
                                            device_id=dev, device_id_type=MESH)

    def flow_out():
        pass_on(z, twin, fcore, fcsend).start()
        for d in range(1, REACH + 1):
            for n, way in enumerate((-1, 1)):
                @pl.when(on_line(z + way * d))
                def _():
                    pass_on(z, line(z + way * d), fnear.at[1 - n, d], fsend.at[n, d]).start()

    def plane_out():
        for c in range(CH):
            for i in range(1, K):
                first_copy(c, i, half).start()
            r1[c][pl.ds(tile * ROWS, ROWS)] = s1[c, me]

    @pl.when(half == 0)
    def _():
        pl.semaphore_wait(barrier, near)
        flow_out()

    @pl.when(half == 1)
    def _():
        pl.semaphore_wait(barrier, near + K)
        for i in range(K):
            pl.semaphore_signal(ready, inc=1, device_id=device(i, 0), device_id_type=MESH)
        send_far()
        flow_out()

    plane_out()
    for d in (4, 1, 2, 3, 5, 6, 7):
        for n, way in enumerate((-1, 1)):
            @pl.when(on_line(z + way * d))
            def _():
                pass_on(z + way * d, twin, fnear.at[n, d], fcsend).wait_recv()
                pass_on(z + way * d, twin, fcore, fcsend).start()
                if d == REACH:
                    for e in range(1, Z - REACH):
                        @pl.when(on_line(z - way * e))
                        def _():
                            pass_on(z + way * d, line(z - way * e), fnear.at[n, d + e], fsend.at[n, d + e]).start()

    @pl.when(half == 0)
    def _():
        pl.semaphore_wait(ready, K)
        send_far()


    all_rows(flow, fcore, Z)

    def turn(t, carry):
        for g in range(2 * Z):
            wide[4 * g:4 * g + 4, :] = flow[g, t]
            wide[64 + 4 * g:68 + 4 * g, :] = flow[g, t]
        for p in range(FW // 128):
            grid[t, p * 128:(p + 1) * 128, :] = wide[:, p * 128:(p + 1) * 128].T
        return carry

    lax.fori_loop(0, T, turn, 0)

    row = lax.broadcasted_iota(jnp.int32, (C, 128), 0)

    def stencil(m_low, c_low, m_high, c_high, scale):
        m_low, m_high = m_low * scale, m_high * scale
        low, high = m_low * (1.0 / 12.0), m_high * (1.0 / 12.0)
        return (
            -low,
            m_low * (7.0 / 12.0 + 0.5 * c_low) + high,
            m_low * (7.0 / 12.0 - 0.5 * c_low) - m_high * (7.0 / 12.0 + 0.5 * c_high),
            -m_high * (7.0 / 12.0 - 0.5 * c_high) - low,
            high,
        )

    def inner_step(t, carry):
        for j in range(C):
            x_low, x_high = grid[t, 9 * j:9 * j + 8, :], grid[t, 9 * j + 1:9 * j + 9, :]
            xc_low, xc_high = grid[t, 72 + 9 * j:80 + 9 * j, :], grid[t, 73 + 9 * j:81 + 9 * j, :]
            y_low, y_high = grid[t, pl.ds(144 + j, 8, stride=9), :], grid[t, pl.ds(145 + j, 8, stride=9), :]
            yc_low, yc_high = grid[t, pl.ds(216 + j, 8, stride=9), :], grid[t, pl.ds(217 + j, 8, stride=9), :]
            thick = grid[t, 288 + 8 * j:296 + 8 * j, :]
            scale = 1.0 / (thick - (x_high - x_low + y_high - y_low))
            xs = stencil(x_low, xc_low, x_high, xc_high, scale)
            ys = stencil(y_low, yc_low, y_high, yc_high, scale)
            centre = thick * scale + xs[2] + ys[2]
            for n, (v, i) in enumerate(((xs[1], 0), (xs[0], 0), (xs[0], 1), (xs[3], 7), (xs[4], 7), (xs[4], 6))):
                kx[t, n, j:j + 1, :] = v[i:i + 1, :]
            for n, (v, at) in enumerate(((ys[1], 0), (ys[0], 0), (ys[0], 1), (ys[3], 7), (ys[4], 7), (ys[4], 6))):
                if at == j:
                    ky[t, n] = v
            xm2 = jnp.where(row >= 2, xs[0], 0.0)
            xm1 = jnp.where(row >= 1, xs[1], 0.0)
            xp1 = jnp.where(row <= 6, xs[3], 0.0)
            xp2 = jnp.where(row <= 5, xs[4], 0.0)
            for c in range(CH):
                lanes = slice(c * 128, (c + 1) * 128)
                v = q[t, j, :, lanes]
                total = centre * v
                total += xm2 * pltpu.roll(v, 2, 0) + xm1 * pltpu.roll(v, 1, 0)
                total += xp1 * pltpu.roll(v, 7, 0) + xp2 * pltpu.roll(v, 6, 0)
                for step, w in ((-2, ys[0]), (-1, ys[1]), (1, ys[3]), (2, ys[4])):
                    if 0 <= j + step < C:
                        total += w * q[t, j + step, :, lanes]
                acc[c, t, 8 * j:8 * j + 8, :] = total
        return carry

    lax.fori_loop(0, T, inner_step, 0)

    def second_copy(c, i):
        return pltpu.make_async_remote_copy(
            src_ref=s2.at[c, ring[i][0]], dst_ref=r2[c].at[pl.ds(me * SIDES, SIDES)], send_sem=ssem2.at[c],
            recv_sem=rsem2.at[c], device_id=device(i, half), device_id_type=MESH)

    for copy in tables:
        copy.wait()

    def collect(c):
        all_rows(r1[c], rsem1.at[c], (2 * K - 1) * ROWS)

        def choose(k, carry):
            home = ((k // 4) * 8 + half * 4 + lax.rem(k, 4)) * T
            for r in range(SIDES):
                s2[c, k, r] = r1[c][pick[r % 4, home + r // 4]]
            return carry

        lax.fori_loop(0, K, choose, 0)

        for i in range(1, K):
            second_copy(c, i).start()
        r2[c][pl.ds(me * SIDES, SIDES)] = s2[c, me]

    def finish(c):
        all_rows(r2[c], rsem2.at[c], (K - 1) * SIDES)

        def lay(t, carry):
            for s in range(4):
                for d in range(2):
                    for a in range(C):
                        halo[t * 4 + s, d, a:a + 1, :] = r2[c][place[d * 8 + a, s, tile * T + t] + 4 * t]
            return carry

        lax.fori_loop(0, T, lay, 0)

        def add(t, carry):
            west, east, south, north = ((halo[t * 4 + s, 0], halo[t * 4 + s, 1]) for s in range(4))
            for (one, two), n, edge, inside in ((west, 0, 0, 1), (east, 3, 7, 6)):
                acc[c, t, pl.ds(edge, 8, stride=8), :] += kx[t, n] * one + kx[t, n + 1] * two
                acc[c, t, pl.ds(inside, 8, stride=8), :] += kx[t, n + 2] * one
            for (one, two), n, edge, inside in ((south, 0, 0, 1), (north, 3, 7, 6)):
                acc[c, t, 8 * edge:8 * edge + 8, :] += ky[t, n] * one + ky[t, n + 1] * two
                acc[c, t, 8 * inside:8 * inside + 8, :] += ky[t, n + 2] * one
            for j in range(C):
                out[t, j, :, c * 128:(c + 1) * 128] = acc[c, t, 8 * j:8 * j + 8, :]
            return carry

        lax.fori_loop(0, T, add, 0)

    for c in range(CH):
        collect(c)
        if c:
            finish(c - 1)
    finish(CH - 1)

    for c in range(CH):
        all_rows(r1[c], ssem1.at[c], (2 * K - 1) * ROWS)
        all_rows(r2[c], ssem2.at[c], (K - 1) * SIDES)
    all_rows(flow, fcsend, Z)
    for n, way in enumerate((-1, 1)):
        for d in range(1, REACH + 1):
            @pl.when(on_line(z + way * d))
            def _():
                pass_on(z, twin, fcore, fsend.at[n, d]).wait_send()

        for e in range(1, Z - REACH):
            @pl.when(on_line(z + way * REACH) & on_line(z - way * e))
            def _():
                pass_on(z, twin, fcore, fsend.at[n, REACH + e]).wait_send()


def shards(tracers, eastward_mass, eastward_courant, northward_mass, northward_courant, thickness, neighbor, orientation):
    f32 = jnp.float32
    vmem, hbm = pl.BlockSpec(memory_space=pltpu.VMEM), pl.BlockSpec(memory_space=pltpu.HBM)
    dma = pltpu.SemaphoreType.DMA
    return pl.pallas_call(
        kernel,
        out_shape=pltpu.VMEM(tracers.shape, f32),
        in_specs=[hbm] * 8,
        out_specs=vmem,
        scratch_shapes=[
            pltpu.VMEM((T, C, C, 384), f32),
            *[pltpu.VMEM((T, C, 4, C + 1), f32)] * 4,
            pltpu.VMEM((T, C, 4, C), f32),
            *[pltpu.VMEM((4, 32 * T), jnp.int32)] * 2,
            dma((10,)),
            pltpu.VMEM((CH, K, ROWS, 1, 128), f32),
            *[pltpu.VMEM((2 * K * ROWS, 1, 128), f32)] * CH,
            pltpu.VMEM((CH, K, SIDES, 1, 128), f32),
            *[pltpu.VMEM((K * SIDES, 1, 128), f32)] * CH,
            pltpu.VMEM((SIDES, 2, C, 128), f32),
            pltpu.VMEM((2 * Z, T, 4, FW), f32),
            pltpu.VMEM((128, FW), f32),
            pltpu.VMEM((T, FW, 128), f32),
            pltpu.VMEM((CH, T, C * C, 128), f32),
            pltpu.VMEM((T, 6, C, 128), f32),
            pltpu.VMEM((T, 6, C, 128), f32),
            pltpu.VMEM((4, 32 * T), jnp.int32),
            pltpu.VMEM((16, 4, 32 * T), jnp.int32),
            pltpu.SMEM((4, 32 * T), jnp.int32),
            pltpu.SMEM((16, 4, 32 * T), jnp.int32),
            pltpu.SemaphoreType.REGULAR,
            dma((CH,)), dma((CH,)), dma((CH,)), dma((CH,)),
            dma((2, Z)), dma((2, Z)), dma, dma,
        ],
        compiler_params=pltpu.CompilerParams(collective_id=0, has_side_effects=True, vmem_limit_bytes=32 * 2**20),
    )(*(pltpu.with_memory_space_constraint(a, pltpu.HBM) for a in (
        tracers,
        eastward_mass.transpose(0, 1, 3, 2),
        eastward_courant.transpose(0, 1, 3, 2),
        northward_mass.transpose(0, 2, 3, 1),
        northward_courant.transpose(0, 2, 3, 1),
        thickness.transpose(0, 1, 3, 2),
        neighbor.T,
        orientation.T,
    )))


def solution(mesh):
    split = P("tile", None, None, "tag")
    return jax.shard_map(
        shards,
        mesh=mesh,
        in_specs=(split,) * 6 + (P(), P()),
        out_specs=split,
        check_vma=False,
    )
```

```python
import jax
import jax.numpy as jnp
from jax import lax
from jax.experimental import pallas as pl
from jax.experimental.pallas import tpu as pltpu
from jax.sharding import PartitionSpec as P

MESH = pl.DeviceIdType.MESH
T = 3
C = 8
GROUPS = ((0, 1), (2,))
PARTS = tuple((n, c) for n, g in enumerate(GROUPS) for c in g)
EARLY = 4
REACH = 4
K = 16
Z = 8
CH = 3
ROWS = 9
SIDES = 12
FW = 384


def collector_cells(k):
    cy, cx, dy, dx = k // 8, k // 4 % 2, k // 2 % 2, k % 2
    far = lambda flag, d: 7 - d if flag else d
    corner = (far(cy, dy), far(cx, dx))
    across_x = (5 - dy if cy else 2 + dy, far(1 - cx, dx))
    across_y = (far(1 - cy, dy), 5 - dx if cx else 2 + dx)
    return corner, across_x, across_y


def kernel(q_in, mx_in, cx_in, my_in, cy_in, th_in, nbr_in, ori_in, out, q, mx, cx_ref, my, cy_ref, th, nbr, ori, load, s1, r1a, r1b, s2, r2a, r2b, halo, flow, wide, grid,
           acc, kx, ky, pick_v, place_v, pick, place, ready, ssem1, rsem1, sfar, rfar, ssem2, rsem2, fnear, fsend, fcore, fcsend):
    r1, r2 = (r1a, r1b), (r2a, r2b)
    tile, tag = lax.axis_index("tile"), lax.axis_index("tag")
    x, half, y = tile // 8, lax.rem(tile // 4, 2), lax.rem(tile, 4)
    me = x * 4 + y
    z, core = tag // 2, lax.rem(tag, 2)
    cy, cx = me // 8, lax.rem(me // 4, 2)

    def line(zz):
        return (tile, zz * 2 + core)

    inputs = [
        pltpu.make_async_copy(src, dst, load.at[n]) for n, (src, dst) in enumerate((
            (q_in, q), (mx_in, mx), (cx_in, cx_ref), (my_in, my), (cy_in, cy_ref), (th_in, th), (nbr_in, nbr), (ori_in, ori)))]
    for copy in inputs:
        copy.start()

    twin = (tile, z * 2 + 1 - core)
    barrier = pltpu.get_barrier_semaphore()

    def greet(dev):
        pl.semaphore_signal(barrier, inc=1, device_id=dev, device_id_type=MESH)

    xs = [jnp.where(x + i < 4, x + i, x + i - 4) for i in range(4)]
    ys = [jnp.where(y + i < 4, y + i, y + i - 4) for i in range(4)]
    ring = [(xs[i // 4] * 4 + ys[i % 4], xs[i // 4] * 8 + ys[i % 4]) for i in range(K)]

    def device(i, h):
        return (ring[i][1] + h * 4, tag)

    for i in range(1, K):
        greet(device(i, half))
    greet(twin)

    early = z < EARLY

    @pl.when(half == 0)
    def _():
        greet(device(0, 1))

        @pl.when(early)
        def _():
            for i in range(1, K):
                greet(device(i, 1))

    def on_line(zz):
        return (zz >= 0) & (zz < Z)

    for d in range(1, REACH + 1):
        for way in (-1, 1):
            @pl.when(on_line(z + way * d))
            def _():
                greet(line(z + way * d))

    near = K + jnp.minimum(z, REACH) + jnp.minimum(Z - 1 - z, REACH)

    def all_rows(ref, sem, rows):
        pltpu.make_async_copy(ref.at[pl.ds(0, rows)], ref.at[pl.ds(0, rows)], sem).wait()

    def stage(t, carry):
        for k in range(K):
            for slot, (j, i) in enumerate(collector_cells(k)):
                for c in range(CH):
                    s1[k, c, t * 3 + slot] = q[t, j, i:i + 1, c * 128:(c + 1) * 128]
        return carry

    inputs[0].wait()
    lax.fori_loop(0, T, stage, 0)

    def first_copy(n, i):
        return pltpu.make_async_remote_copy(
            src_ref=s1.at[ring[i][0], pl.ds(GROUPS[n][0], len(GROUPS[n]))], dst_ref=r1[n].at[me], send_sem=ssem1.at[n],
            recv_sem=rsem1.at[n], device_id=device(i, half), device_id_type=MESH)

    def far_copy(n, c):
        at = c - GROUPS[n][0]
        return pltpu.make_async_remote_copy(
            src_ref=r1[n].at[pl.ds(0, K), at], dst_ref=r1[n].at[pl.ds(K, K), at], send_sem=sfar.at[c],
            recv_sem=rfar.at[c], device_id=device(0, 1 - half), device_id_type=MESH)

    def early_copy(n, c, i):
        return pltpu.make_async_remote_copy(
            src_ref=s1.at[ring[i][0], c], dst_ref=r1[n].at[K + me, c - GROUPS[n][0]], send_sem=sfar.at[c], recv_sem=rfar.at[c],
            device_id=device(i, 0), device_id_type=MESH)

    def send_far():
        for n in range(len(GROUPS)):
            all_rows(r1[n], rsem1.at[n], K - 1)

        @pl.when((half == 0) | jnp.logical_not(early))
        def _():
            for n, c in PARTS:
                far_copy(n, c).start()

    def block(zz):
        return flow.at[zz * 2 + core]

    def pass_on(zz, dev, sem, done):
        return pltpu.make_async_remote_copy(src_ref=block(zz), dst_ref=block(zz), send_sem=done, recv_sem=sem,
                                            device_id=dev, device_id_type=MESH)

    def flow_out():
        pass_on(z, twin, fcore, fcsend).start()
        for d in range(1, REACH + 1):
            for n, way in enumerate((-1, 1)):
                @pl.when(on_line(z + way * d))
                def _():
                    pass_on(z, line(z + way * d), fnear.at[1 - n, d], fsend.at[n, d]).start()

    def plane_out():
        for n in range(len(GROUPS)):
            for i in range(1, K):
                first_copy(n, i).start()
        for n, c in PARTS:
            r1[n][me, c - GROUPS[n][0]] = s1[me, c]

    @pl.when(half == 0)
    def _():
        pl.semaphore_wait(barrier, near)

    @pl.when(half == 1)
    def _():
        pl.semaphore_wait(barrier, near + jnp.where(early, K, 1))
        pl.semaphore_signal(ready, inc=1, device_id=device(0, 0), device_id_type=MESH)

        @pl.when(early)
        def _():
            for n, c in PARTS:
                for i in range(K):
                    early_copy(n, c, i).start()

    def pack(t, carry):
        flow[tag, t] = jnp.zeros((4, FW), jnp.float32)
        for j in range(C):
            for n, ref in enumerate((mx, cx_ref, my, cy_ref)):
                at = n * 72 + j * 9
                flow[tag, t, :, at:at + 9] = ref[t, j]
            at = 288 + j * 8
            flow[tag, t, :, at:at + 8] = th[t, j]
        return carry

    for copy in inputs[1:6]:
        copy.wait()
    lax.fori_loop(0, T, pack, 0)

    flow_out()
    plane_out()

    inputs[6].wait()
    inputs[7].wait()
    code = ori[...]
    flip, b, is_y = code & 1, (code >> 1) & 1, code >> 2 == 1
    slot = jnp.where(is_y, jnp.where(b == cy, 0, 2), jnp.where(b == cx, 0, 1))
    home = (nbr[...] * 171) >> 9
    away = jnp.where(((home >> 2) & 1) == half, 0, K)
    pick_v[...] = (away + (home >> 3) * 4 + (home & 3)) * 16 + (nbr[...] - 3 * home) * 3 + slot
    for d in range(2):
        for a in range(C):
            a2, a1, a0 = a // 4, a // 2 % 2, a % 2
            end = 1 - flip if a2 else flip
            cross = 1 - b if a1 != a2 else b
            deep = a0 ^ a2
            kx_at = end * 8 + cross * 4 + deep * 2 + d
            ky_at = cross * 8 + end * 4 + d * 2 + deep
            place_v[d * 8 + a] = jnp.where(is_y, ky_at, kx_at)
    tables = [pltpu.make_async_copy(pick_v, pick, load.at[8]), pltpu.make_async_copy(place_v, place, load.at[9])]
    for copy in tables:
        copy.start()

    @pl.when(half == 1)
    def _():
        send_far()

    for d in (4, 1, 2, 3, 5, 6, 7):
        for n, way in enumerate((-1, 1)):
            @pl.when(on_line(z + way * d))
            def _():
                pass_on(z + way * d, twin, fnear.at[n, d], fcsend).wait_recv()
                pass_on(z + way * d, twin, fcore, fcsend).start()
                if d == REACH:
                    for e in range(1, Z - REACH):
                        @pl.when(on_line(z - way * e))
                        def _():
                            pass_on(z + way * d, line(z - way * e), fnear.at[n, d + e], fsend.at[n, d + e]).start()

    @pl.when((half == 0) & jnp.logical_not(((z != 2) & (z != 1))))
    def _():
        pl.semaphore_wait(ready, 1)
        send_far()

    all_rows(flow, fcore, Z)

    def turn(t, carry):
        for g in range(2 * Z):
            wide[4 * g:4 * g + 4, :] = flow[g, t]
            wide[64 + 4 * g:68 + 4 * g, :] = flow[g, t]
        for p in range(FW // 128):
            grid[t, p * 128:(p + 1) * 128, :] = wide[:, p * 128:(p + 1) * 128].T
        return carry

    lax.fori_loop(0, T, turn, 0)

    row = lax.broadcasted_iota(jnp.int32, (C, 128), 0)

    def stencil(m_low, c_low, m_high, c_high, scale):
        m_low, m_high = m_low * scale, m_high * scale
        low, high = m_low * (1.0 / 12.0), m_high * (1.0 / 12.0)
        return (
            -low,
            m_low * (7.0 / 12.0 + 0.5 * c_low) + high,
            m_low * (7.0 / 12.0 - 0.5 * c_low) - m_high * (7.0 / 12.0 + 0.5 * c_high),
            -m_high * (7.0 / 12.0 - 0.5 * c_high) - low,
            high,
        )

    def inner_step(t, carry):
        for j in range(C):
            x_low, x_high = grid[t, 9 * j:9 * j + 8, :], grid[t, 9 * j + 1:9 * j + 9, :]
            xc_low, xc_high = grid[t, 72 + 9 * j:80 + 9 * j, :], grid[t, 73 + 9 * j:81 + 9 * j, :]
            y_low, y_high = grid[t, pl.ds(144 + j, 8, stride=9), :], grid[t, pl.ds(145 + j, 8, stride=9), :]
            yc_low, yc_high = grid[t, pl.ds(216 + j, 8, stride=9), :], grid[t, pl.ds(217 + j, 8, stride=9), :]
            thick = grid[t, 288 + 8 * j:296 + 8 * j, :]
            scale = 1.0 / (thick - (x_high - x_low + y_high - y_low))
            xs = stencil(x_low, xc_low, x_high, xc_high, scale)
            ys = stencil(y_low, yc_low, y_high, yc_high, scale)
            centre = thick * scale + xs[2] + ys[2]
            for n, (v, i) in enumerate(((xs[1], 0), (xs[0], 0), (xs[0], 1), (xs[3], 7), (xs[4], 7), (xs[4], 6))):
                kx[t, n, j:j + 1, :] = v[i:i + 1, :]
            for n, (v, at) in enumerate(((ys[1], 0), (ys[0], 0), (ys[0], 1), (ys[3], 7), (ys[4], 7), (ys[4], 6))):
                if at == j:
                    ky[t, n] = v
            xm2 = jnp.where(row >= 2, xs[0], 0.0)
            xm1 = jnp.where(row >= 1, xs[1], 0.0)
            xp1 = jnp.where(row <= 6, xs[3], 0.0)
            xp2 = jnp.where(row <= 5, xs[4], 0.0)
            for c in range(CH):
                lanes = slice(c * 128, (c + 1) * 128)
                v = q[t, j, :, lanes]
                total = centre * v
                total += xm2 * pltpu.roll(v, 2, 0) + xm1 * pltpu.roll(v, 1, 0)
                total += xp1 * pltpu.roll(v, 7, 0) + xp2 * pltpu.roll(v, 6, 0)
                for step, w in ((-2, ys[0]), (-1, ys[1]), (1, ys[3]), (2, ys[4])):
                    if 0 <= j + step < C:
                        total += w * q[t, j + step, :, lanes]
                acc[c, t, 8 * j:8 * j + 8, :] = total
        return carry

    lax.fori_loop(0, T, inner_step, 0)

    @pl.when((half == 0) & ((z != 2) & (z != 1)))
    def _():
        pl.semaphore_wait(ready, 1)
        send_far()

    def second_copy(n, i):
        cs = pl.ds(GROUPS[n][0], len(GROUPS[n]))
        return pltpu.make_async_remote_copy(
            src_ref=s2.at[ring[i][0], cs], dst_ref=r2[n].at[me], send_sem=ssem2.at[n], recv_sem=rsem2.at[n],
            device_id=device(i, half), device_id_type=MESH)

    def second_wait(n, sem):
        part = r2[n].at[pl.ds(0, K - 1)]
        pltpu.make_async_copy(part, part, sem.at[n]).wait()

    for copy in tables:
        copy.wait()

    def collect(n):
        for c in GROUPS[n]:
            far_copy(n, c).wait_recv()

        def choose(k, carry):
            home = ((k // 4) * 8 + half * 4 + lax.rem(k, 4)) * T
            for r in range(SIDES):
                at = pick[r % 4, home + r // 4]
                for c in GROUPS[n]:
                    s2[k, c, r] = r1[n][at >> 4, c - GROUPS[n][0], at & 15]
            return carry

        lax.fori_loop(0, K, choose, 0)
        for i in range(1, K):
            second_copy(n, i).start()
        for c in GROUPS[n]:
            r2[n][me, c - GROUPS[n][0]] = s2[me, c]

    def finish(n, c):
        def lay(t, carry):
            for s in range(4):
                for d in range(2):
                    for a in range(C):
                        halo[t * 4 + s, d, a:a + 1, :] = r2[n][place[d * 8 + a, s, tile * T + t], c - GROUPS[n][0], 4 * t + s]
            return carry

        lax.fori_loop(0, T, lay, 0)

        def add(t, carry):
            west, east, south, north = ((halo[t * 4 + s, 0], halo[t * 4 + s, 1]) for s in range(4))
            for (one, two), n, edge, inside in ((west, 0, 0, 1), (east, 3, 7, 6)):
                acc[c, t, pl.ds(edge, 8, stride=8), :] += kx[t, n] * one + kx[t, n + 1] * two
                acc[c, t, pl.ds(inside, 8, stride=8), :] += kx[t, n + 2] * one
            for (one, two), n, edge, inside in ((south, 0, 0, 1), (north, 3, 7, 6)):
                acc[c, t, 8 * edge:8 * edge + 8, :] += ky[t, n] * one + ky[t, n + 1] * two
                acc[c, t, 8 * inside:8 * inside + 8, :] += ky[t, n + 2] * one
            for j in range(C):
                out[t, j, :, c * 128:(c + 1) * 128] = acc[c, t, 8 * j:8 * j + 8, :]
            return carry

        lax.fori_loop(0, T, add, 0)

    def close(n):
        second_wait(n, rsem2)
        for c in GROUPS[n]:
            finish(n, c)

    for n in range(len(GROUPS)):
        collect(n)
        if n:
            close(n - 1)
    close(len(GROUPS) - 1)

    for n in range(len(GROUPS)):
        all_rows(r1[n], ssem1.at[n], K - 1)
    for n, c in PARTS:
        far_copy(n, c).wait_send()
    for n in range(len(GROUPS)):
        second_wait(n, ssem2)
    all_rows(flow, fcsend, Z)
    for n, way in enumerate((-1, 1)):
        for d in range(1, REACH + 1):
            @pl.when(on_line(z + way * d))
            def _():
                pass_on(z, twin, fcore, fsend.at[n, d]).wait_send()

        for e in range(1, Z - REACH):
            @pl.when(on_line(z + way * REACH) & on_line(z - way * e))
            def _():
                pass_on(z, twin, fcore, fsend.at[n, REACH + e]).wait_send()


def shards(tracers, eastward_mass, eastward_courant, northward_mass, northward_courant, thickness, neighbor, orientation):
    f32 = jnp.float32
    vmem, hbm = pl.BlockSpec(memory_space=pltpu.VMEM), pl.BlockSpec(memory_space=pltpu.HBM)
    dma = pltpu.SemaphoreType.DMA
    return pl.pallas_call(
        kernel,
        out_shape=pltpu.VMEM(tracers.shape, f32),
        in_specs=[hbm] * 8,
        out_specs=vmem,
        scratch_shapes=[
            pltpu.VMEM((T, C, C, 384), f32),
            *[pltpu.VMEM((T, C, 4, C + 1), f32)] * 4,
            pltpu.VMEM((T, C, 4, C), f32),
            *[pltpu.VMEM((4, 32 * T), jnp.int32)] * 2,
            dma((10,)),
            pltpu.VMEM((K, CH, ROWS, 1, 128), f32),
            *[pltpu.VMEM((2 * K, len(g), ROWS, 1, 128), f32) for g in GROUPS],
            pltpu.VMEM((K, CH, SIDES, 1, 128), f32),
            *[pltpu.VMEM((K, len(g), SIDES, 1, 128), f32) for g in GROUPS],
            pltpu.VMEM((SIDES, 2, C, 128), f32),
            pltpu.VMEM((2 * Z, T, 4, FW), f32),
            pltpu.VMEM((128, FW), f32),
            pltpu.VMEM((T, FW, 128), f32),
            pltpu.VMEM((CH, T, C * C, 128), f32),
            pltpu.VMEM((T, 6, C, 128), f32),
            pltpu.VMEM((T, 6, C, 128), f32),
            pltpu.VMEM((4, 32 * T), jnp.int32),
            pltpu.VMEM((16, 4, 32 * T), jnp.int32),
            pltpu.SMEM((4, 32 * T), jnp.int32),
            pltpu.SMEM((16, 4, 32 * T), jnp.int32),
            pltpu.SemaphoreType.REGULAR,
            *[dma((CH,))] * 6,
            dma((2, Z)), dma((2, Z)), dma, dma,
        ],
        compiler_params=pltpu.CompilerParams(collective_id=0, has_side_effects=True, vmem_limit_bytes=32 * 2**20),
    )(*(pltpu.with_memory_space_constraint(a, pltpu.HBM) for a in (
        tracers,
        eastward_mass.transpose(0, 1, 3, 2),
        eastward_courant.transpose(0, 1, 3, 2),
        northward_mass.transpose(0, 2, 3, 1),
        northward_courant.transpose(0, 2, 3, 1),
        thickness.transpose(0, 1, 3, 2),
        neighbor.T,
        orientation.T,
    )))


def solution(mesh):
    split = P("tile", None, None, "tag")
    return jax.shard_map(
        shards,
        mesh=mesh,
        in_specs=(split,) * 6 + (P(), P()),
        out_specs=split,
        check_vma=False,
    )
```

```python
import jax
import jax.numpy as jnp
from jax import lax
from jax.experimental import pallas as pl
from jax.experimental.pallas import tpu as pltpu
from jax.sharding import PartitionSpec as P

MESH = pl.DeviceIdType.MESH
T = 3
C = 8
GROUPS = ((0, 1), (2,))
PARTS = tuple((n, c) for n, g in enumerate(GROUPS) for c in g)
EARLY = 5
REACH = 4
K = 16
Z = 8
CH = 3
ROWS = 9
SIDES = 12
FW = 384


def collector_cells(k):
    cy, cx, dy, dx = k // 8, k // 4 % 2, k // 2 % 2, k % 2
    far = lambda flag, d: 7 - d if flag else d
    corner = (far(cy, dy), far(cx, dx))
    across_x = (5 - dy if cy else 2 + dy, far(1 - cx, dx))
    across_y = (far(1 - cy, dy), 5 - dx if cx else 2 + dx)
    return corner, across_x, across_y


def kernel(q_in, mx_in, cx_in, my_in, cy_in, th_in, nbr_in, ori_in, out, q, mx, cx_ref, my, cy_ref, th, nbr, ori, load, s1, r1a, r1b, s2, r2a, r2b, halo, flow, wide, grid,
           acc, kx, ky, pick_v, place_v, pick, place, ready, ssem1, rsem1, sfar, rfar, ssem2, rsem2, fnear, fsend, fcore, fcsend):
    r1, r2 = (r1a, r1b), (r2a, r2b)
    tile, tag = lax.axis_index("tile"), lax.axis_index("tag")
    x, half, y = tile // 8, lax.rem(tile // 4, 2), lax.rem(tile, 4)
    me = x * 4 + y
    z, core = tag // 2, lax.rem(tag, 2)
    cy, cx = me // 8, lax.rem(me // 4, 2)

    def line(zz):
        return (tile, zz * 2 + core)

    inputs = [
        pltpu.make_async_copy(src, dst, load.at[n]) for n, (src, dst) in enumerate((
            (q_in, q), (mx_in, mx), (cx_in, cx_ref), (my_in, my), (cy_in, cy_ref), (th_in, th), (nbr_in, nbr), (ori_in, ori)))]
    for copy in inputs:
        copy.start()

    twin = (tile, z * 2 + 1 - core)
    barrier = pltpu.get_barrier_semaphore()

    def greet(dev):
        pl.semaphore_signal(barrier, inc=1, device_id=dev, device_id_type=MESH)

    xs = [jnp.where(x + i < 4, x + i, x + i - 4) for i in range(4)]
    ys = [jnp.where(y + i < 4, y + i, y + i - 4) for i in range(4)]
    ring = [(xs[i // 4] * 4 + ys[i % 4], xs[i // 4] * 8 + ys[i % 4]) for i in range(K)]

    def device(i, h):
        return (ring[i][1] + h * 4, tag)

    for i in range(1, K):
        greet(device(i, half))
    greet(twin)

    early = z < EARLY

    @pl.when(half == 0)
    def _():
        greet(device(0, 1))

        @pl.when(early)
        def _():
            for i in range(1, K):
                greet(device(i, 1))

    def on_line(zz):
        return (zz >= 0) & (zz < Z)

    for d in range(1, REACH + 1):
        for way in (-1, 1):
            @pl.when(on_line(z + way * d))
            def _():
                greet(line(z + way * d))

    near = K + jnp.minimum(z, REACH) + jnp.minimum(Z - 1 - z, REACH)

    def all_rows(ref, sem, rows):
        pltpu.make_async_copy(ref.at[pl.ds(0, rows)], ref.at[pl.ds(0, rows)], sem).wait()

    def stage(t, carry):
        for k in range(K):
            for slot, (j, i) in enumerate(collector_cells(k)):
                for c in range(CH):
                    s1[k, c, t * 3 + slot] = q[t, j, i:i + 1, c * 128:(c + 1) * 128]
        return carry

    inputs[0].wait()
    lax.fori_loop(0, T, stage, 0)

    def first_copy(n, i):
        return pltpu.make_async_remote_copy(
            src_ref=s1.at[ring[i][0], pl.ds(GROUPS[n][0], len(GROUPS[n]))], dst_ref=r1[n].at[me], send_sem=ssem1.at[n],
            recv_sem=rsem1.at[n], device_id=device(i, half), device_id_type=MESH)

    def far_copy(n):
        return pltpu.make_async_remote_copy(
            src_ref=r1[n].at[pl.ds(0, K)], dst_ref=r1[n].at[pl.ds(K, K)], send_sem=sfar.at[n], recv_sem=rfar.at[n],
            device_id=device(0, 1 - half), device_id_type=MESH)

    def early_copy(n, i):
        return pltpu.make_async_remote_copy(
            src_ref=s1.at[ring[i][0], pl.ds(GROUPS[n][0], len(GROUPS[n]))], dst_ref=r1[n].at[K + me], send_sem=sfar.at[n],
            recv_sem=rfar.at[n], device_id=device(i, 0), device_id_type=MESH)

    def send_far():
        for n in range(len(GROUPS)):
            all_rows(r1[n], rsem1.at[n], K - 1)

        @pl.when((half == 0) | jnp.logical_not(early))
        def _():
            for n in range(len(GROUPS)):
                far_copy(n).start()

    def block(zz):
        return flow.at[zz * 2 + core]

    def pass_on(zz, dev, sem, done):
        return pltpu.make_async_remote_copy(src_ref=block(zz), dst_ref=block(zz), send_sem=done, recv_sem=sem,
                                            device_id=dev, device_id_type=MESH)

    def flow_out():
        pass_on(z, twin, fcore, fcsend).start()
        for d in range(1, REACH + 1):
            for n, way in enumerate((-1, 1)):
                @pl.when(on_line(z + way * d))
                def _():
                    pass_on(z, line(z + way * d), fnear.at[1 - n, d], fsend.at[n, d]).start()

    def plane_out():
        for n in range(len(GROUPS)):
            for i in range(1, K):
                first_copy(n, i).start()
        for n, c in PARTS:
            r1[n][me, c - GROUPS[n][0]] = s1[me, c]

    @pl.when(half == 0)
    def _():
        pl.semaphore_wait(barrier, near)

    @pl.when(half == 1)
    def _():
        pl.semaphore_wait(barrier, near + jnp.where(early, K, 1))
        pl.semaphore_signal(ready, inc=1, device_id=device(0, 0), device_id_type=MESH)

        @pl.when(early)
        def _():
            for n in range(len(GROUPS)):
                for i in range(K):
                    early_copy(n, i).start()

    def pack(t, carry):
        flow[tag, t] = jnp.zeros((4, FW), jnp.float32)
        for j in range(C):
            for n, ref in enumerate((mx, cx_ref, my, cy_ref)):
                at = n * 72 + j * 9
                flow[tag, t, :, at:at + 9] = ref[t, j]
            at = 288 + j * 8
            flow[tag, t, :, at:at + 8] = th[t, j]
        return carry

    for copy in inputs[1:6]:
        copy.wait()
    lax.fori_loop(0, T, pack, 0)

    flow_out()
    plane_out()

    inputs[6].wait()
    inputs[7].wait()
    code = ori[...]
    flip, b, is_y = code & 1, (code >> 1) & 1, code >> 2 == 1
    slot = jnp.where(is_y, jnp.where(b == cy, 0, 2), jnp.where(b == cx, 0, 1))
    home = (nbr[...] * 171) >> 9
    away = jnp.where(((home >> 2) & 1) == half, 0, K)
    pick_v[...] = (away + (home >> 3) * 4 + (home & 3)) * 16 + (nbr[...] - 3 * home) * 3 + slot
    for d in range(2):
        for a in range(C):
            a2, a1, a0 = a // 4, a // 2 % 2, a % 2
            end = 1 - flip if a2 else flip
            cross = 1 - b if a1 != a2 else b
            deep = a0 ^ a2
            kx_at = end * 8 + cross * 4 + deep * 2 + d
            ky_at = cross * 8 + end * 4 + d * 2 + deep
            place_v[d * 8 + a] = jnp.where(is_y, ky_at, kx_at)
    tables = [pltpu.make_async_copy(pick_v, pick, load.at[8]), pltpu.make_async_copy(place_v, place, load.at[9])]
    for copy in tables:
        copy.start()

    @pl.when(half == 1)
    def _():
        send_far()

    for d in (4, 1, 2, 3, 5, 6, 7):
        for n, way in enumerate((-1, 1)):
            @pl.when(on_line(z + way * d))
            def _():
                pass_on(z + way * d, twin, fnear.at[n, d], fcsend).wait_recv()
                pass_on(z + way * d, twin, fcore, fcsend).start()
                if d == REACH:
                    for e in range(1, Z - REACH):
                        @pl.when(on_line(z - way * e))
                        def _():
                            pass_on(z + way * d, line(z - way * e), fnear.at[n, d + e], fsend.at[n, d + e]).start()

    @pl.when((half == 0) & jnp.logical_not(((z != 2) & (z != 1))))
    def _():
        pl.semaphore_wait(ready, 1)
        send_far()

    all_rows(flow, fcore, Z)

    def turn(t, carry):
        for g in range(2 * Z):
            wide[4 * g:4 * g + 4, :] = flow[g, t]
            wide[64 + 4 * g:68 + 4 * g, :] = flow[g, t]
        for p in range(FW // 128):
            grid[t, p * 128:(p + 1) * 128, :] = wide[:, p * 128:(p + 1) * 128].T
        return carry

    lax.fori_loop(0, T, turn, 0)

    row = lax.broadcasted_iota(jnp.int32, (C, 128), 0)

    def stencil(m_low, c_low, m_high, c_high, scale):
        m_low, m_high = m_low * scale, m_high * scale
        low, high = m_low * (1.0 / 12.0), m_high * (1.0 / 12.0)
        return (
            -low,
            m_low * (7.0 / 12.0 + 0.5 * c_low) + high,
            m_low * (7.0 / 12.0 - 0.5 * c_low) - m_high * (7.0 / 12.0 + 0.5 * c_high),
            -m_high * (7.0 / 12.0 - 0.5 * c_high) - low,
            high,
        )

    def inner_step(t, carry):
        for j in range(C):
            x_low, x_high = grid[t, 9 * j:9 * j + 8, :], grid[t, 9 * j + 1:9 * j + 9, :]
            xc_low, xc_high = grid[t, 72 + 9 * j:80 + 9 * j, :], grid[t, 73 + 9 * j:81 + 9 * j, :]
            y_low, y_high = grid[t, pl.ds(144 + j, 8, stride=9), :], grid[t, pl.ds(145 + j, 8, stride=9), :]
            yc_low, yc_high = grid[t, pl.ds(216 + j, 8, stride=9), :], grid[t, pl.ds(217 + j, 8, stride=9), :]
            thick = grid[t, 288 + 8 * j:296 + 8 * j, :]
            scale = 1.0 / (thick - (x_high - x_low + y_high - y_low))
            xs = stencil(x_low, xc_low, x_high, xc_high, scale)
            ys = stencil(y_low, yc_low, y_high, yc_high, scale)
            centre = thick * scale + xs[2] + ys[2]
            for n, (v, i) in enumerate(((xs[1], 0), (xs[0], 0), (xs[0], 1), (xs[3], 7), (xs[4], 7), (xs[4], 6))):
                kx[t, n, j:j + 1, :] = v[i:i + 1, :]
            for n, (v, at) in enumerate(((ys[1], 0), (ys[0], 0), (ys[0], 1), (ys[3], 7), (ys[4], 7), (ys[4], 6))):
                if at == j:
                    ky[t, n] = v
            xm2 = jnp.where(row >= 2, xs[0], 0.0)
            xm1 = jnp.where(row >= 1, xs[1], 0.0)
            xp1 = jnp.where(row <= 6, xs[3], 0.0)
            xp2 = jnp.where(row <= 5, xs[4], 0.0)
            for c in range(CH):
                lanes = slice(c * 128, (c + 1) * 128)
                v = q[t, j, :, lanes]
                total = centre * v
                total += xm2 * pltpu.roll(v, 2, 0) + xm1 * pltpu.roll(v, 1, 0)
                total += xp1 * pltpu.roll(v, 7, 0) + xp2 * pltpu.roll(v, 6, 0)
                for step, w in ((-2, ys[0]), (-1, ys[1]), (1, ys[3]), (2, ys[4])):
                    if 0 <= j + step < C:
                        total += w * q[t, j + step, :, lanes]
                acc[c, t, 8 * j:8 * j + 8, :] = total
        return carry

    lax.fori_loop(0, T, inner_step, 0)

    @pl.when((half == 0) & ((z != 2) & (z != 1)))
    def _():
        pl.semaphore_wait(ready, 1)
        send_far()

    def second_copy(n, i):
        cs = pl.ds(GROUPS[n][0], len(GROUPS[n]))
        return pltpu.make_async_remote_copy(
            src_ref=s2.at[ring[i][0], cs], dst_ref=r2[n].at[me], send_sem=ssem2.at[n], recv_sem=rsem2.at[n],
            device_id=device(i, half), device_id_type=MESH)

    def second_wait(n, sem):
        part = r2[n].at[pl.ds(0, K - 1)]
        pltpu.make_async_copy(part, part, sem.at[n]).wait()

    for copy in tables:
        copy.wait()

    def collect(n):
        far_copy(n).wait_recv()

        def choose(k, carry):
            home = ((k // 4) * 8 + half * 4 + lax.rem(k, 4)) * T
            for r in range(SIDES):
                at = pick[r % 4, home + r // 4]
                for c in GROUPS[n]:
                    s2[k, c, r] = r1[n][at >> 4, c - GROUPS[n][0], at & 15]
            return carry

        lax.fori_loop(0, K, choose, 0)
        for i in range(1, K):
            second_copy(n, i).start()
        for c in GROUPS[n]:
            r2[n][me, c - GROUPS[n][0]] = s2[me, c]

    def finish(n, c):
        def lay(t, carry):
            for s in range(4):
                for d in range(2):
                    for a in range(C):
                        halo[t * 4 + s, d, a:a + 1, :] = r2[n][place[d * 8 + a, s, tile * T + t], c - GROUPS[n][0], 4 * t + s]
            return carry

        lax.fori_loop(0, T, lay, 0)

        def add(t, carry):
            west, east, south, north = ((halo[t * 4 + s, 0], halo[t * 4 + s, 1]) for s in range(4))
            for (one, two), n, edge, inside in ((west, 0, 0, 1), (east, 3, 7, 6)):
                acc[c, t, pl.ds(edge, 8, stride=8), :] += kx[t, n] * one + kx[t, n + 1] * two
                acc[c, t, pl.ds(inside, 8, stride=8), :] += kx[t, n + 2] * one
            for (one, two), n, edge, inside in ((south, 0, 0, 1), (north, 3, 7, 6)):
                acc[c, t, 8 * edge:8 * edge + 8, :] += ky[t, n] * one + ky[t, n + 1] * two
                acc[c, t, 8 * inside:8 * inside + 8, :] += ky[t, n + 2] * one
            for j in range(C):
                out[t, j, :, c * 128:(c + 1) * 128] = acc[c, t, 8 * j:8 * j + 8, :]
            return carry

        lax.fori_loop(0, T, add, 0)

    def close(n):
        second_wait(n, rsem2)
        for c in GROUPS[n]:
            finish(n, c)

    for n in range(len(GROUPS)):
        collect(n)
        if n:
            close(n - 1)
    close(len(GROUPS) - 1)

    for n in range(len(GROUPS)):
        all_rows(r1[n], ssem1.at[n], K - 1)
        far_copy(n).wait_send()
    for n in range(len(GROUPS)):
        second_wait(n, ssem2)
    all_rows(flow, fcsend, Z)
    for n, way in enumerate((-1, 1)):
        for d in range(1, REACH + 1):
            @pl.when(on_line(z + way * d))
            def _():
                pass_on(z, twin, fcore, fsend.at[n, d]).wait_send()

        for e in range(1, Z - REACH):
            @pl.when(on_line(z + way * REACH) & on_line(z - way * e))
            def _():
                pass_on(z, twin, fcore, fsend.at[n, REACH + e]).wait_send()


def shards(tracers, eastward_mass, eastward_courant, northward_mass, northward_courant, thickness, neighbor, orientation):
    f32 = jnp.float32
    vmem, hbm = pl.BlockSpec(memory_space=pltpu.VMEM), pl.BlockSpec(memory_space=pltpu.HBM)
    dma = pltpu.SemaphoreType.DMA
    return pl.pallas_call(
        kernel,
        out_shape=pltpu.VMEM(tracers.shape, f32),
        in_specs=[hbm] * 8,
        out_specs=vmem,
        scratch_shapes=[
            pltpu.VMEM((T, C, C, 384), f32),
            *[pltpu.VMEM((T, C, 4, C + 1), f32)] * 4,
            pltpu.VMEM((T, C, 4, C), f32),
            *[pltpu.VMEM((4, 32 * T), jnp.int32)] * 2,
            dma((10,)),
            pltpu.VMEM((K, CH, ROWS, 1, 128), f32),
            *[pltpu.VMEM((2 * K, len(g), ROWS, 1, 128), f32) for g in GROUPS],
            pltpu.VMEM((K, CH, SIDES, 1, 128), f32),
            *[pltpu.VMEM((K, len(g), SIDES, 1, 128), f32) for g in GROUPS],
            pltpu.VMEM((SIDES, 2, C, 128), f32),
            pltpu.VMEM((2 * Z, T, 4, FW), f32),
            pltpu.VMEM((128, FW), f32),
            pltpu.VMEM((T, FW, 128), f32),
            pltpu.VMEM((CH, T, C * C, 128), f32),
            pltpu.VMEM((T, 6, C, 128), f32),
            pltpu.VMEM((T, 6, C, 128), f32),
            pltpu.VMEM((4, 32 * T), jnp.int32),
            pltpu.VMEM((16, 4, 32 * T), jnp.int32),
            pltpu.SMEM((4, 32 * T), jnp.int32),
            pltpu.SMEM((16, 4, 32 * T), jnp.int32),
            pltpu.SemaphoreType.REGULAR,
            *[dma((CH,))] * 6,
            dma((2, Z)), dma((2, Z)), dma, dma,
        ],
        compiler_params=pltpu.CompilerParams(collective_id=0, has_side_effects=True, vmem_limit_bytes=32 * 2**20),
    )(*(pltpu.with_memory_space_constraint(a, pltpu.HBM) for a in (
        tracers,
        eastward_mass.transpose(0, 1, 3, 2),
        eastward_courant.transpose(0, 1, 3, 2),
        northward_mass.transpose(0, 2, 3, 1),
        northward_courant.transpose(0, 2, 3, 1),
        thickness.transpose(0, 1, 3, 2),
        neighbor.T,
        orientation.T,
    )))


def solution(mesh):
    split = P("tile", None, None, "tag")
    return jax.shard_map(
        shards,
        mesh=mesh,
        in_specs=(split,) * 6 + (P(), P()),
        out_specs=split,
        check_vma=False,
    )
```

```python
import jax
import jax.numpy as jnp
from jax import lax
from jax.experimental import pallas as pl
from jax.experimental.pallas import tpu as pltpu
from jax.sharding import PartitionSpec as P

MESH = pl.DeviceIdType.MESH
T = 3
C = 8
GROUPS = ((0, 1), (2,))
PARTS = tuple((n, c) for n, g in enumerate(GROUPS) for c in g)
EARLY = 5
REACH = 4
K = 16
FAR_FIRST = sorted(range(1, K), key=lambda i: -min(i // 4, 4 - i // 4) - min(i % 4, 4 - i % 4))
Z = 8
CH = 3
ROWS = 9
SIDES = 12
FW = 384


def collector_cells(k):
    cy, cx, dy, dx = k // 8, k // 4 % 2, k // 2 % 2, k % 2
    far = lambda flag, d: 7 - d if flag else d
    corner = (far(cy, dy), far(cx, dx))
    across_x = (5 - dy if cy else 2 + dy, far(1 - cx, dx))
    across_y = (far(1 - cy, dy), 5 - dx if cx else 2 + dx)
    return corner, across_x, across_y


def kernel(q_in, mx_in, cx_in, my_in, cy_in, th_in, nbr_in, ori_in, out, q, mx, cx_ref, my, cy_ref, th, nbr, ori, load, s1, r1a, r1b, s2, r2a, r2b, halo, flow, wide, grid,
           acc, kx, ky, pick_v, place_v, pick, place, ready, ssem1, rsem1, sfar, rfar, ssem2, rsem2, fnear, fsend, fcore, fcsend):
    r1, r2 = (r1a, r1b), (r2a, r2b)
    tile, tag = lax.axis_index("tile"), lax.axis_index("tag")
    x, half, y = tile // 8, lax.rem(tile // 4, 2), lax.rem(tile, 4)
    me = x * 4 + y
    z, core = tag // 2, lax.rem(tag, 2)
    cy, cx = me // 8, lax.rem(me // 4, 2)

    def line(zz):
        return (tile, zz * 2 + core)

    inputs = [
        pltpu.make_async_copy(src, dst, load.at[n]) for n, (src, dst) in enumerate((
            (q_in, q), (mx_in, mx), (cx_in, cx_ref), (my_in, my), (cy_in, cy_ref), (th_in, th), (nbr_in, nbr), (ori_in, ori)))]
    for copy in inputs:
        copy.start()

    twin = (tile, z * 2 + 1 - core)
    barrier = pltpu.get_barrier_semaphore()

    def greet(dev):
        pl.semaphore_signal(barrier, inc=1, device_id=dev, device_id_type=MESH)

    xs = [jnp.where(x + i < 4, x + i, x + i - 4) for i in range(4)]
    ys = [jnp.where(y + i < 4, y + i, y + i - 4) for i in range(4)]
    ring = [(xs[i // 4] * 4 + ys[i % 4], xs[i // 4] * 8 + ys[i % 4]) for i in range(K)]

    def device(i, h):
        return (ring[i][1] + h * 4, tag)

    for i in range(1, K):
        greet(device(i, half))
    greet(twin)

    early = z < EARLY

    @pl.when(half == 0)
    def _():
        greet(device(0, 1))

        @pl.when(early)
        def _():
            for i in range(1, K):
                greet(device(i, 1))

    def on_line(zz):
        return (zz >= 0) & (zz < Z)

    for d in range(1, REACH + 1):
        for way in (-1, 1):
            @pl.when(on_line(z + way * d))
            def _():
                greet(line(z + way * d))

    near = K + jnp.minimum(z, REACH) + jnp.minimum(Z - 1 - z, REACH)

    def all_rows(ref, sem, rows):
        pltpu.make_async_copy(ref.at[pl.ds(0, rows)], ref.at[pl.ds(0, rows)], sem).wait()

    def stage(t, carry):
        for k in range(K):
            for slot, (j, i) in enumerate(collector_cells(k)):
                for c in range(CH):
                    s1[k, c, t * 3 + slot] = q[t, j, i:i + 1, c * 128:(c + 1) * 128]
        return carry

    inputs[0].wait()
    lax.fori_loop(0, T, stage, 0)

    def first_copy(n, i):
        return pltpu.make_async_remote_copy(
            src_ref=s1.at[ring[i][0], pl.ds(GROUPS[n][0], len(GROUPS[n]))], dst_ref=r1[n].at[me], send_sem=ssem1.at[n],
            recv_sem=rsem1.at[n], device_id=device(i, half), device_id_type=MESH)

    def far_copy(n):
        return pltpu.make_async_remote_copy(
            src_ref=r1[n].at[pl.ds(0, K)], dst_ref=r1[n].at[pl.ds(K, K)], send_sem=sfar.at[n], recv_sem=rfar.at[n],
            device_id=device(0, 1 - half), device_id_type=MESH)

    def early_copy(n, i):
        return pltpu.make_async_remote_copy(
            src_ref=s1.at[ring[i][0], pl.ds(GROUPS[n][0], len(GROUPS[n]))], dst_ref=r1[n].at[K + me], send_sem=sfar.at[n],
            recv_sem=rfar.at[n], device_id=device(i, 0), device_id_type=MESH)

    def send_far():
        for n in range(len(GROUPS)):
            all_rows(r1[n], rsem1.at[n], K - 1)

        @pl.when((half == 0) | jnp.logical_not(early))
        def _():
            for n in range(len(GROUPS)):
                far_copy(n).start()

    def block(zz):
        return flow.at[zz * 2 + core]

    def pass_on(zz, dev, sem, done):
        return pltpu.make_async_remote_copy(src_ref=block(zz), dst_ref=block(zz), send_sem=done, recv_sem=sem,
                                            device_id=dev, device_id_type=MESH)

    def flow_out():
        pass_on(z, twin, fcore, fcsend).start()
        for d in range(1, REACH + 1):
            for n, way in enumerate((-1, 1)):
                @pl.when(on_line(z + way * d))
                def _():
                    pass_on(z, line(z + way * d), fnear.at[1 - n, d], fsend.at[n, d]).start()

    def plane_out():
        for n in range(len(GROUPS)):
            for i in FAR_FIRST:
                first_copy(n, i).start()
        for n, c in PARTS:
            r1[n][me, c - GROUPS[n][0]] = s1[me, c]

    @pl.when(half == 0)
    def _():
        pl.semaphore_wait(barrier, near)

    @pl.when(half == 1)
    def _():
        pl.semaphore_wait(barrier, near + jnp.where(early, K, 1))
        pl.semaphore_signal(ready, inc=1, device_id=device(0, 0), device_id_type=MESH)

        @pl.when(early)
        def _():
            for n in range(len(GROUPS)):
                for i in range(K):
                    early_copy(n, i).start()

    def pack(t, carry):
        flow[tag, t] = jnp.zeros((4, FW), jnp.float32)
        for j in range(C):
            for n, ref in enumerate((mx, cx_ref, my, cy_ref)):
                at = n * 72 + j * 9
                flow[tag, t, :, at:at + 9] = ref[t, j]
            at = 288 + j * 8
            flow[tag, t, :, at:at + 8] = th[t, j]
        return carry

    for copy in inputs[1:6]:
        copy.wait()
    lax.fori_loop(0, T, pack, 0)

    flow_out()
    plane_out()

    inputs[6].wait()
    inputs[7].wait()
    code = ori[...]
    flip, b, is_y = code & 1, (code >> 1) & 1, code >> 2 == 1
    slot = jnp.where(is_y, jnp.where(b == cy, 0, 2), jnp.where(b == cx, 0, 1))
    home = (nbr[...] * 171) >> 9
    away = jnp.where(((home >> 2) & 1) == half, 0, K)
    pick_v[...] = (away + (home >> 3) * 4 + (home & 3)) * 16 + (nbr[...] - 3 * home) * 3 + slot
    for d in range(2):
        for a in range(C):
            a2, a1, a0 = a // 4, a // 2 % 2, a % 2
            end = 1 - flip if a2 else flip
            cross = 1 - b if a1 != a2 else b
            deep = a0 ^ a2
            kx_at = end * 8 + cross * 4 + deep * 2 + d
            ky_at = cross * 8 + end * 4 + d * 2 + deep
            place_v[d * 8 + a] = jnp.where(is_y, ky_at, kx_at)
    tables = [pltpu.make_async_copy(pick_v, pick, load.at[8]), pltpu.make_async_copy(place_v, place, load.at[9])]
    for copy in tables:
        copy.start()

    @pl.when(half == 1)
    def _():
        send_far()

    for d in (4, 1, 2, 3, 5, 6, 7):
        for n, way in enumerate((-1, 1)):
            @pl.when(on_line(z + way * d))
            def _():
                pass_on(z + way * d, twin, fnear.at[n, d], fcsend).wait_recv()
                pass_on(z + way * d, twin, fcore, fcsend).start()
                if d == REACH:
                    for e in range(1, Z - REACH):
                        @pl.when(on_line(z - way * e))
                        def _():
                            pass_on(z + way * d, line(z - way * e), fnear.at[n, d + e], fsend.at[n, d + e]).start()

    @pl.when((half == 0) & jnp.logical_not(((z != 2) & (z != 1))))
    def _():
        pl.semaphore_wait(ready, 1)
        send_far()

    all_rows(flow, fcore, Z)

    def turn(t, carry):
        for g in range(2 * Z):
            wide[4 * g:4 * g + 4, :] = flow[g, t]
            wide[64 + 4 * g:68 + 4 * g, :] = flow[g, t]
        for p in range(FW // 128):
            grid[t, p * 128:(p + 1) * 128, :] = wide[:, p * 128:(p + 1) * 128].T
        return carry

    lax.fori_loop(0, T, turn, 0)

    row = lax.broadcasted_iota(jnp.int32, (C, 128), 0)

    def stencil(m_low, c_low, m_high, c_high, scale):
        m_low, m_high = m_low * scale, m_high * scale
        low, high = m_low * (1.0 / 12.0), m_high * (1.0 / 12.0)
        return (
            -low,
            m_low * (7.0 / 12.0 + 0.5 * c_low) + high,
            m_low * (7.0 / 12.0 - 0.5 * c_low) - m_high * (7.0 / 12.0 + 0.5 * c_high),
            -m_high * (7.0 / 12.0 - 0.5 * c_high) - low,
            high,
        )

    def inner_step(t, carry):
        for j in range(C):
            x_low, x_high = grid[t, 9 * j:9 * j + 8, :], grid[t, 9 * j + 1:9 * j + 9, :]
            xc_low, xc_high = grid[t, 72 + 9 * j:80 + 9 * j, :], grid[t, 73 + 9 * j:81 + 9 * j, :]
            y_low, y_high = grid[t, pl.ds(144 + j, 8, stride=9), :], grid[t, pl.ds(145 + j, 8, stride=9), :]
            yc_low, yc_high = grid[t, pl.ds(216 + j, 8, stride=9), :], grid[t, pl.ds(217 + j, 8, stride=9), :]
            thick = grid[t, 288 + 8 * j:296 + 8 * j, :]
            scale = 1.0 / (thick - (x_high - x_low + y_high - y_low))
            xs = stencil(x_low, xc_low, x_high, xc_high, scale)
            ys = stencil(y_low, yc_low, y_high, yc_high, scale)
            centre = thick * scale + xs[2] + ys[2]
            for n, (v, i) in enumerate(((xs[1], 0), (xs[0], 0), (xs[0], 1), (xs[3], 7), (xs[4], 7), (xs[4], 6))):
                kx[t, n, j:j + 1, :] = v[i:i + 1, :]
            for n, (v, at) in enumerate(((ys[1], 0), (ys[0], 0), (ys[0], 1), (ys[3], 7), (ys[4], 7), (ys[4], 6))):
                if at == j:
                    ky[t, n] = v
            xm2 = jnp.where(row >= 2, xs[0], 0.0)
            xm1 = jnp.where(row >= 1, xs[1], 0.0)
            xp1 = jnp.where(row <= 6, xs[3], 0.0)
            xp2 = jnp.where(row <= 5, xs[4], 0.0)
            for c in range(CH):
                lanes = slice(c * 128, (c + 1) * 128)
                v = q[t, j, :, lanes]
                total = centre * v
                total += xm2 * pltpu.roll(v, 2, 0) + xm1 * pltpu.roll(v, 1, 0)
                total += xp1 * pltpu.roll(v, 7, 0) + xp2 * pltpu.roll(v, 6, 0)
                for step, w in ((-2, ys[0]), (-1, ys[1]), (1, ys[3]), (2, ys[4])):
                    if 0 <= j + step < C:
                        total += w * q[t, j + step, :, lanes]
                acc[c, t, 8 * j:8 * j + 8, :] = total
        return carry

    lax.fori_loop(0, T, inner_step, 0)

    @pl.when((half == 0) & ((z != 2) & (z != 1)))
    def _():
        pl.semaphore_wait(ready, 1)
        send_far()

    def second_copy(n, i):
        cs = pl.ds(GROUPS[n][0], len(GROUPS[n]))
        return pltpu.make_async_remote_copy(
            src_ref=s2.at[ring[i][0], cs], dst_ref=r2[n].at[me], send_sem=ssem2.at[n], recv_sem=rsem2.at[n],
            device_id=device(i, half), device_id_type=MESH)

    def second_wait(n, sem):
        part = r2[n].at[pl.ds(0, K - 1)]
        pltpu.make_async_copy(part, part, sem.at[n]).wait()

    for copy in tables:
        copy.wait()

    def collect(n):
        far_copy(n).wait_recv()

        def choose(k, carry):
            home = ((k // 4) * 8 + half * 4 + lax.rem(k, 4)) * T
            for r in range(SIDES):
                at = pick[r % 4, home + r // 4]
                for c in GROUPS[n]:
                    s2[k, c, r] = r1[n][at >> 4, c - GROUPS[n][0], at & 15]
            return carry

        lax.fori_loop(0, K, choose, 0)
        for i in FAR_FIRST:
            second_copy(n, i).start()
        for c in GROUPS[n]:
            r2[n][me, c - GROUPS[n][0]] = s2[me, c]

    def finish(n, c):
        def lay(t, carry):
            for s in range(4):
                for d in range(2):
                    for a in range(C):
                        halo[t * 4 + s, d, a:a + 1, :] = r2[n][place[d * 8 + a, s, tile * T + t], c - GROUPS[n][0], 4 * t + s]
            return carry

        lax.fori_loop(0, T, lay, 0)

        def add(t, carry):
            west, east, south, north = ((halo[t * 4 + s, 0], halo[t * 4 + s, 1]) for s in range(4))
            for (one, two), n, edge, inside in ((west, 0, 0, 1), (east, 3, 7, 6)):
                acc[c, t, pl.ds(edge, 8, stride=8), :] += kx[t, n] * one + kx[t, n + 1] * two
                acc[c, t, pl.ds(inside, 8, stride=8), :] += kx[t, n + 2] * one
            for (one, two), n, edge, inside in ((south, 0, 0, 1), (north, 3, 7, 6)):
                acc[c, t, 8 * edge:8 * edge + 8, :] += ky[t, n] * one + ky[t, n + 1] * two
                acc[c, t, 8 * inside:8 * inside + 8, :] += ky[t, n + 2] * one
            for j in range(C):
                out[t, j, :, c * 128:(c + 1) * 128] = acc[c, t, 8 * j:8 * j + 8, :]
            return carry

        lax.fori_loop(0, T, add, 0)

    def close(n):
        second_wait(n, rsem2)
        for c in GROUPS[n]:
            finish(n, c)

    for n in range(len(GROUPS)):
        collect(n)
        if n:
            close(n - 1)
    close(len(GROUPS) - 1)

    for n in range(len(GROUPS)):
        all_rows(r1[n], ssem1.at[n], K - 1)
        far_copy(n).wait_send()
    for n in range(len(GROUPS)):
        second_wait(n, ssem2)
    all_rows(flow, fcsend, Z)
    for n, way in enumerate((-1, 1)):
        for d in range(1, REACH + 1):
            @pl.when(on_line(z + way * d))
            def _():
                pass_on(z, twin, fcore, fsend.at[n, d]).wait_send()

        for e in range(1, Z - REACH):
            @pl.when(on_line(z + way * REACH) & on_line(z - way * e))
            def _():
                pass_on(z, twin, fcore, fsend.at[n, REACH + e]).wait_send()


def shards(tracers, eastward_mass, eastward_courant, northward_mass, northward_courant, thickness, neighbor, orientation):
    f32 = jnp.float32
    vmem, hbm = pl.BlockSpec(memory_space=pltpu.VMEM), pl.BlockSpec(memory_space=pltpu.HBM)
    dma = pltpu.SemaphoreType.DMA
    return pl.pallas_call(
        kernel,
        out_shape=pltpu.VMEM(tracers.shape, f32),
        in_specs=[hbm] * 8,
        out_specs=vmem,
        scratch_shapes=[
            pltpu.VMEM((T, C, C, 384), f32),
            *[pltpu.VMEM((T, C, 4, C + 1), f32)] * 4,
            pltpu.VMEM((T, C, 4, C), f32),
            *[pltpu.VMEM((4, 32 * T), jnp.int32)] * 2,
            dma((10,)),
            pltpu.VMEM((K, CH, ROWS, 1, 128), f32),
            *[pltpu.VMEM((2 * K, len(g), ROWS, 1, 128), f32) for g in GROUPS],
            pltpu.VMEM((K, CH, SIDES, 1, 128), f32),
            *[pltpu.VMEM((K, len(g), SIDES, 1, 128), f32) for g in GROUPS],
            pltpu.VMEM((SIDES, 2, C, 128), f32),
            pltpu.VMEM((2 * Z, T, 4, FW), f32),
            pltpu.VMEM((128, FW), f32),
            pltpu.VMEM((T, FW, 128), f32),
            pltpu.VMEM((CH, T, C * C, 128), f32),
            pltpu.VMEM((T, 6, C, 128), f32),
            pltpu.VMEM((T, 6, C, 128), f32),
            pltpu.VMEM((4, 32 * T), jnp.int32),
            pltpu.VMEM((16, 4, 32 * T), jnp.int32),
            pltpu.SMEM((4, 32 * T), jnp.int32),
            pltpu.SMEM((16, 4, 32 * T), jnp.int32),
            pltpu.SemaphoreType.REGULAR,
            *[dma((CH,))] * 6,
            dma((2, Z)), dma((2, Z)), dma, dma,
        ],
        compiler_params=pltpu.CompilerParams(collective_id=0, has_side_effects=True, vmem_limit_bytes=32 * 2**20),
    )(*(pltpu.with_memory_space_constraint(a, pltpu.HBM) for a in (
        tracers,
        eastward_mass.transpose(0, 1, 3, 2),
        eastward_courant.transpose(0, 1, 3, 2),
        northward_mass.transpose(0, 2, 3, 1),
        northward_courant.transpose(0, 2, 3, 1),
        thickness.transpose(0, 1, 3, 2),
        neighbor.T,
        orientation.T,
    )))


def solution(mesh):
    split = P("tile", None, None, "tag")
    return jax.shard_map(
        shards,
        mesh=mesh,
        in_specs=(split,) * 6 + (P(), P()),
        out_specs=split,
        check_vma=False,
    )
```
